32 devices in a mesh: groups: 2 (over y), blk: 4 (over z), fsdp: 2 (over x), sub: 2 (over core).
Axes of the slice: x: 2, y: 2, z: 4, core: 2. Of those that a mesh axis runs over, the one named last changes fastest.
Arguments:
- grad_out: bfloat16 [2048, 8192], P(('groups', 'blk'), 'sub'), parts along dimension 0, may hold values from -6 to 6
- inputs: bfloat16 [2048, 8192], P(('groups', 'blk'), ('fsdp', 'sub')), parts along dimension 0, may hold values from -6 to 6
- gate_act: bfloat16 [2048, 14336], P(('groups', 'blk'), ('fsdp', 'sub')), parts along dimension 0, may hold values from -6 to 6
- w_down: bfloat16 [14336, 8192], P(('fsdp', 'sub'), 'blk'), may hold values from -0.0625 to 0.0625
- proj_in: bfloat16 [8192, 64], P(('fsdp', 'sub')), may hold values from -0.0625 to 0.0625
- proj_out: bfloat16 [14336, 64], P(('fsdp', 'sub')), may hold values from -0.046875 to 0.046875
- queries: bfloat16 [8, 16, 4096], P(('groups', 'blk'), 'fsdp', 'sub'), parts along dimension 0, may hold values from -0.015625 to 0.015625
- example_of: int32 [2048], P(('groups', 'blk')), parts along dimension 0, may hold values from 0 to 7, as said below
Outputs:
- sketches: bfloat16 [64, 4096], P(('groups', 'blk'), 'sub'), parts along dimension 0
- scores: float32 [64, 4, 16], P(('groups', 'blk'), None, ('fsdp', 'sub')), parts along dimension 0
The draws below stay inside these ranges and needn't reach their ends.
There are 2 independent parts, one for each index of `groups`. The reference program is written for one: setup_inputs(seed, part) draws one part's arguments, and reference() takes and returns one part's arrays. A program takes and returns all parts, laid end to end along the dimension named above; an argument that names none is the same for every part. Nothing has to cross between parts.
Inputs may be any that keep to these rules, and one draw needn't show every extreme that they name: `example_of`: within each aligned block of 256 tokens the numbers never fall and each of 0 to 7 appears.
All inputs are finite; a program needn't handle non-finite values.
Results may differ from the reference program's by a relative error of at most 0.0032.
Values may be sent and summed in bfloat16 or wider, within the bound.
No kernel may reach another device: no remote copies, remote signals or barrier semaphores. Data moves between devices by JAX's collectives and lax.ppermute only.
A program may use at most 192 MiB of HBM per device.

```python
import jax
import jax.numpy as jnp
from jax import lax

D = 8192
FFW = 14336
R = 64
TOK_DEV = 256
EX_DEV = 8
TOKENS = 1024
EXAMPLES = 32
QF = 16
N_BLK = 4


def draw_example_of(key, part):
    key = jax.random.fold_in(key, 7)
    keys = jax.random.split(key, TOKENS // TOK_DEV)

    def one_block(block_key):
        cuts = jax.random.permutation(block_key, TOK_DEV - 1)[:EX_DEV - 1] + 1
        places = jnp.arange(TOK_DEV, dtype=jnp.int32)
        return jnp.sum((places[:, None] >= cuts[None, :]).astype(jnp.int32), axis=1)
    return jax.vmap(one_block)(keys).reshape(-1).astype(jnp.int32)


def steps_of(stream_key, extent, cuts, low, high):
    def one(dim, parts):
        steps = jax.random.uniform(jax.random.fold_in(jax.random.fold_in(stream_key, 6), dim), (parts,), jnp.float32, low / len(cuts), high / len(cuts))
        return jnp.repeat(jnp.exp(steps), extent[dim] // parts).reshape((-1,) + (1,) * (len(extent) - dim - 1))

    factor_of = one(*cuts[0])
    for cut in cuts[1:]:
        factor_of = factor_of * one(*cut)
    return factor_of


def noise(own_key, shape, scale, bound, shards=(), held_as=jnp.bfloat16):
    loudness = steps_of(own_key, shape, shards, -0.22, 0.18) if shards else 1.0
    entries = jax.random.normal(own_key, shape, jnp.float32) * scale * loudness
    return jnp.minimum(jnp.maximum(entries, -bound), bound).astype(held_as)


def setup_inputs(seed: int = 0, part: int = 0) -> dict:
    key_list = jax.random.split(jax.random.key(seed), 9)
    own_keys = jax.random.split(jax.random.fold_in(key_list[8], part), 9)
    grad_out = noise(own_keys[0], (TOKENS, D), 1.0, 6.0, ((0, 4), (1, 2)))
    inputs = noise(own_keys[1], (TOKENS, D), 1.0, 6.0, ((0, 4), (1, 4)))
    gate_act = noise(own_keys[2], (TOKENS, FFW), 1.0, 6.0, ((0, 4), (1, 4)))
    w_down = noise(key_list[3], (FFW, D), D ** -0.5, 0.0625, ((0, 4), (1, 4)))
    proj_in = noise(key_list[4], (D, R), D ** -0.5, 0.0625, ((0, 4),))
    proj_out = noise(key_list[5], (FFW, R), FFW ** -0.5, 0.046875, ((0, 4),))
    queries = noise(own_keys[6], (N_BLK, QF, R * R), (R * R * TOK_DEV // EX_DEV) ** -0.5, 0.015625, ((0, 4), (1, 2), (2, 2)))
    example_of = draw_example_of(jax.random.fold_in(jax.random.fold_in(key_list[8], part), 71), part)
    return {"grad_out": grad_out, "inputs": inputs, "gate_act": gate_act, "w_down": w_down, "proj_in": proj_in, "proj_out": proj_out, "queries": queries, "example_of": example_of}


def reference(grad_out, inputs, gate_act, w_down, proj_in, proj_out, queries, example_of):
    xp = jnp.dot(inputs, proj_in, preferred_element_type=jnp.float32)
    proj32 = proj_out.astype(jnp.float32)

    def one_block(index):
        start = index * TOK_DEV
        grads = lax.dynamic_slice_in_dim(grad_out, start, TOK_DEV, 0)
        gates = lax.dynamic_slice_in_dim(gate_act, start, TOK_DEV, 0)
        hidden_grad = jnp.dot(grads, w_down.T, preferred_element_type=jnp.float32)
        up_proj = jnp.dot(hidden_grad * gates.astype(jnp.float32), proj32, precision=lax.Precision.HIGHEST)
        left = lax.dynamic_slice_in_dim(xp, start, TOK_DEV, 0)
        owners = lax.dynamic_slice_in_dim(example_of, start, TOK_DEV, 0)
        onehot = (owners[:, None] == jnp.arange(EX_DEV, dtype=jnp.int32)[None, :]).astype(jnp.float32)
        weighted = (onehot[:, :, None] * left[:, None, :]).reshape(TOK_DEV, EX_DEV * R)
        return jnp.dot(weighted.T, up_proj, precision=lax.Precision.HIGHEST).reshape(EX_DEV, R * R)

    stacked = lax.map(one_block, jnp.arange(N_BLK, dtype=jnp.int32))
    sketches = stacked.reshape(EXAMPLES, R * R).astype(jnp.bfloat16)
    flat_queries = queries.reshape(N_BLK * QF, R * R)
    scores = jnp.dot(sketches, flat_queries.T, preferred_element_type=jnp.float32)
    return sketches, scores.reshape(EXAMPLES, N_BLK, QF)
```

```python
import jax
import jax.numpy as jnp
from jax import lax
from jax.sharding import PartitionSpec as P

R = 64
EX_DEV = 8
CHUNKS = 2
F32 = jnp.float32
BF16 = jnp.bfloat16


def line_right(block):
    n = lax.axis_size("blk")
    return lax.ppermute(block, "blk", [(i, i + 1) for i in range(n - 1)])


def line_left(block):
    n = lax.axis_size("blk")
    return lax.ppermute(block, "blk", [(i + 1, i) for i in range(n - 1)])


def shifted(block, axis, distance):
    n = lax.axis_size(axis)
    return lax.ppermute(block, axis, [(i, (i + distance) % n) for i in range(n)])


def gathered(block, axis):
    n = lax.axis_size(axis)
    if n == 1:
        return block[None]
    here = lax.axis_index(axis)
    got = [block] + [shifted(block, axis, e) for e in range(1, n)]
    return jnp.stack([lax.select_n((here - i) % n, *got) for i in range(n)])


def summed(block, axes):
    for axis in axes:
        n = lax.axis_size(axis)
        step = 1
        while step < n:
            block = block + lax.ppermute(block, axis, [(i, i ^ step) for i in range(n)])
            step *= 2
    return block


def local(grad_out, inputs, gate_act, w_down, proj_in, proj_out, queries, example_of):
    n = lax.axis_size("blk")
    cores = lax.axis_size("sub")
    n_f = lax.axis_size("fsdp")
    z, x, core = lax.axis_index("blk"), lax.axis_index("fsdp"), lax.axis_index("sub")
    tok = grad_out.shape[0]
    hid, dblk = w_down.shape
    group = n // cores
    rows = tok // n_f
    half = tok // 2
    part = half // CHUNKS
    proj32 = proj_out.astype(F32)

    def project(block):
        return jnp.dot(block, proj32, precision=lax.Precision.HIGH)

    def features(p):
        mine = lax.dynamic_slice(grad_out, (x * rows, ((z + p) % group) * dblk), (rows, dblk))
        route = []
        for zs in range(n):
            for cs in range(cores):
                zd = cs * group + (zs + p) % group
                route.append((zs * cores + cs, zd * cores + zs // group))
        got = lax.ppermute(mine, ("blk", "sub"), route)
        whole = gathered(got, "fsdp").reshape(tok, dblk)
        return gathered(whole, "sub")

    order = list(range(1, group)) + [0]
    grads = {p: features(p) for p in order}

    hidden = {
        p: lax.dot_general(
            grads[p].reshape(cores * tok, dblk),
            w_down,
            (((1,), (1,)), ((), ())),
            preferred_element_type=F32,
        ).reshape(cores, tok, hid)
        for p in order
    }

    def hidden_of(distance, start, size):
        which = ((z - distance) % n) // group
        return lax.dynamic_slice(hidden[distance % group], (which, start, 0), (1, size, hid))[0]

    gates = {k: [] for k in range(1, n)}
    up_second = []
    for c in range(CHUNKS):
        own = gate_act[c * part : (c + 1) * part]
        from_left, from_right = [line_right(own)], [line_left(own)]
        for s in range(1, n):
            start = half + c * part
            mine = hidden_of(s, start, part)
            payload = from_left[-1].astype(F32) + jnp.where(z < s, mine, 0.0)
            from_left.append(line_right(payload.astype(BF16)))
            mine = hidden_of(n - s, start, part)
            payload = from_right[-1].astype(F32) + jnp.where(z + s >= n, mine, 0.0)
            from_right.append(line_left(payload.astype(BF16)))
        for k in range(1, n):
            gates[k].append(jnp.where(z >= k, from_left[k - 1], from_right[n - 1 - k]))
        total = hidden_of(0, start, part) + from_left[-1].astype(F32) + from_right[-1].astype(F32)
        up = project(total * gate_act[start : start + part].astype(F32))
        up_second.append(summed(up, ("sub", "fsdp")))

    up_first = project(hidden_of(0, 0, half) * gate_act[:half].astype(F32))
    for k in range(1, n):
        gate = jnp.concatenate(gates[k])
        up = project(hidden_of(k, 0, half) * gate.astype(F32))
        up_first = up_first + shifted(up, "blk", -k)
    up_first = summed(up_first, ("sub", "fsdp"))
    up_proj = jnp.concatenate([up_first] + up_second)

    left_proj = summed(
        jnp.dot(inputs, proj_in, preferred_element_type=F32), ("sub", "fsdp")
    )
    onehot = (example_of[:, None] == jnp.arange(EX_DEV, dtype=jnp.int32)[None, :]).astype(F32)
    weighted = (onehot[:, :, None] * left_proj[:, None, :]).reshape(tok, EX_DEV * R)
    full_sketch = lax.dot_general(
        weighted, up_proj, (((0,), (0,)), ((), ())), precision=lax.Precision.HIGHEST
    )
    sketch = full_sketch.reshape(EX_DEV, R * R).astype(BF16)
    width = R * R // cores
    sketch_part = lax.dynamic_slice(sketch, (0, core * width), (EX_DEV, width))

    own_q = queries[0].reshape(cores, -1, width)
    got_q = [lax.dynamic_index_in_dim(own_q, core, 0, keepdims=False)]
    for e in range(1, cores):
        got_q.append(
            shifted(lax.dynamic_index_in_dim(own_q, (core + e) % cores, 0, keepdims=False), "sub", e)
        )
    own_q = jnp.concatenate([lax.select_n((core - i) % cores, *got_q) for i in range(cores)], axis=1)
    all_q = gathered(own_q, "blk")
    scores = lax.dot_general(
        sketch, all_q, (((1,), (2,)), ((), ())), preferred_element_type=F32
    )
    return sketch_part, scores


def solution(mesh):
    in_specs = (
        P(("groups", "blk"), "sub"),
        P(("groups", "blk"), ("fsdp", "sub")),
        P(("groups", "blk"), ("fsdp", "sub")),
        P(("fsdp", "sub"), "blk"),
        P(("fsdp", "sub"), None),
        P(("fsdp", "sub"), None),
        P(("groups", "blk"), "fsdp", "sub"),
        P(("groups", "blk")),
    )
    out_specs = (P(("groups", "blk"), "sub"), P(("groups", "blk"), None, ("fsdp", "sub")))
    return jax.shard_map(local, mesh=mesh, in_specs=in_specs, out_specs=out_specs, check_vma=False)
```

```python
import jax
import jax.numpy as jnp
from jax import lax
from jax.experimental import pallas as pl
from jax.experimental.pallas import tpu as pltpu
from jax.sharding import PartitionSpec as P

R = 64
EX_DEV = 8
LANES = 128
CHUNKS = 2
FIRST_LIMIT = 56
PAYLOAD_LIMIT = 12
F32 = jnp.float32
BF16 = jnp.bfloat16
ROWS_ROWS = (((1,), (1,)), ((), ()))
ANYWHERE = pl.BlockSpec(memory_space=pl.ANY)


def line_right(block):
    n = lax.axis_size("blk")
    return lax.ppermute(block, "blk", [(i, i + 1) for i in range(n - 1)])


def line_left(block):
    n = lax.axis_size("blk")
    return lax.ppermute(block, "blk", [(i + 1, i) for i in range(n - 1)])


def onward(block, reverse):
    n, n_f = lax.axis_size("blk"), lax.axis_size("fsdp")
    route = []
    for z in range(n):
        for x in range(n_f):
            to = z + (1 if (x % 2 == 0) != reverse else -1)
            route.append((z * n_f + x, to * n_f + x if 0 <= to < n else z * n_f + (x ^ 1)))
    return lax.ppermute(block, ("blk", "fsdp"), route)


def shifted(block, axis, distance):
    n = lax.axis_size(axis)
    return lax.ppermute(block, axis, [(i, (i + distance) % n) for i in range(n)])


def gathered(block, axis):
    n = lax.axis_size(axis)
    if n == 1:
        return block[None]
    here = lax.axis_index(axis)
    got = [block] + [shifted(block, axis, e) for e in range(1, n)]
    return jnp.stack([lax.select_n((here - i) % n, *got) for i in range(n)])


def summed(block, axes):
    for axis in axes:
        n = lax.axis_size(axis)
        step = 1
        while step < n:
            block = block + lax.ppermute(block, axis, [(i, i ^ step) for i in range(n)])
            step *= 2
    return block


def block_of(size, most):
    return max(b for b in range(LANES, most + 1, LANES) if size % b == 0)


def split(block):
    high = block.astype(BF16)
    return high, (block - high.astype(F32)).astype(BF16)


SHORT = pl.CostEstimate(flops=1000, bytes_accessed=1000, transcendentals=0)


def cost(microseconds):
    return pl.CostEstimate(
        flops=1000, bytes_accessed=3_690_000 * microseconds, transcendentals=0
    )


def stack_kernel(*refs):
    out_ref = refs[-1]
    for i, ref in enumerate(refs[:-2]):
        out_ref[i] = ref[...]


def hidden_grad(blocks, w_down, start, rows, after):
    depth = blocks[0].shape[1]
    stacked = pl.pallas_call(
        stack_kernel,
        grid=(1,),
        in_specs=[pl.BlockSpec((rows, depth), lambda i: (start // rows, 0))] * len(blocks)
        + [ANYWHERE],
        out_specs=pl.BlockSpec((len(blocks), rows, depth), lambda i: (0, 0, 0)),
        out_shape=jax.ShapeDtypeStruct((len(blocks), rows, depth), BF16),
        compiler_params=pltpu.CompilerParams(vmem_limit_bytes=16 << 20),
        cost_estimate=cost(1),
        name="stack",
    )(*blocks, after)
    out = lax.dot_general(
        stacked.reshape(-1, depth), w_down, ROWS_ROWS, preferred_element_type=F32
    )
    return out.reshape(len(blocks), rows, -1)


def join_kernel(n, s_ref, *refs):
    blocks, out_ref = refs[:n], refs[-1]
    rows = blocks[0].shape[0]
    for e, block in enumerate(blocks):
        start = pl.multiple_of(lax.rem(s_ref[0] + n - e, n) * rows, rows)
        out_ref[pl.ds(start, rows), :] = block[...]


def join(blocks, here, after):
    n = len(blocks)
    rows, depth = blocks[0].shape
    whole = pl.BlockSpec((rows, depth), lambda i, s: (0, 0))

    def kernel(*refs):
        join_kernel(n, *refs)

    return pl.pallas_call(
        kernel,
        grid_spec=pltpu.PrefetchScalarGridSpec(
            num_scalar_prefetch=1,
            grid=(1,),
            in_specs=[whole] * n + [ANYWHERE] * len(after),
            out_specs=pl.BlockSpec((n * rows, depth), lambda i, s: (0, 0)),
        ),
        out_shape=jax.ShapeDtypeStruct((n * rows, depth), BF16),
        compiler_params=pltpu.CompilerParams(vmem_limit_bytes=12 << 20),
        cost_estimate=SHORT,
        name="join",
    )(here.reshape(1), *blocks, *after)


def copy_kernel(s_ref, block_ref, after_ref, out_ref):
    del s_ref, after_ref
    out_ref[...] = block_ref[...]


def block_copy(array, row, column, shape, after):
    grid_spec = pltpu.PrefetchScalarGridSpec(
        num_scalar_prefetch=1,
        grid=(1,),
        in_specs=[pl.BlockSpec(shape, lambda i, s: (s[0], s[1])), ANYWHERE],
        out_specs=pl.BlockSpec(shape, lambda i, s: (0, 0)),
    )
    return pl.pallas_call(
        copy_kernel,
        grid_spec=grid_spec,
        out_shape=jax.ShapeDtypeStruct(shape, array.dtype),
        compiler_params=pltpu.CompilerParams(vmem_limit_bytes=12 << 20),
        cost_estimate=cost(1),
        name="block_copy",
    )(jnp.stack([row, column]).astype(jnp.int32), array, after)


def payload_kernel(n_got, n_mine, s_ref, *refs):
    got, mine, out_ref = refs[:n_got], refs[n_got : n_got + n_mine], refs[-1]
    rows = got[0].shape[0]
    each = n_got // (out_ref.shape[0] // rows)
    for c in range(n_got // each):
        at = pl.ds(c * rows, rows)
        term = mine[0][0, at, :]
        if n_mine == 2:
            term = jnp.where(s_ref[4] > 0, mine[1][0, at, :], term)
        came = got[c * each][...]
        if each == 2:
            came = jnp.where(s_ref[4] > 0, got[c * each + 1][...], came)
        came = jnp.where(s_ref[2] > 0, came.astype(F32), 0.0)
        out_ref[at, :] = (came + jnp.where(s_ref[3] > 0, term, 0.0)).astype(BF16)


def payload(scalars, got, parts, hidden, rows_at, after):
    part, hid = got[0].shape
    rows = part * parts
    step = block_of(hid, 1792)
    grid_spec = pltpu.PrefetchScalarGridSpec(
        num_scalar_prefetch=1,
        grid=(hid // step,),
        in_specs=[pl.BlockSpec((part, step), lambda i, s: (0, i))] * len(got)
        + [
            pl.BlockSpec((1, rows, step), lambda i, s, j=j: (s[j], rows_at[j] // rows, i))
            for j in range(len(hidden))
        ]
        + [ANYWHERE],
        out_specs=pl.BlockSpec((rows, step), lambda i, s: (0, i)),
    )

    def kernel(*refs):
        payload_kernel(len(got), len(hidden), *refs)

    return pl.pallas_call(
        kernel,
        grid_spec=grid_spec,
        out_shape=jax.ShapeDtypeStruct((rows, hid), BF16),
        compiler_params=pltpu.CompilerParams(vmem_limit_bytes=PAYLOAD_LIMIT << 20),
        cost_estimate=SHORT,
        name="payload",
    )(scalars, *got, *hidden, after)


def first_kernel(n, cores, s_ref, own_gate, proj, *refs):
    group = n // cores
    held, out_ref = refs[-2 - group : -2], refs[-1]
    gates = [
        jnp.concatenate([ref[...] for ref in refs[i * CHUNKS : (i + 1) * CHUNKS]])
        for i in range(2 * n - 2)
    ]

    @pl.when(pl.program_id(0) == 0)
    def _():
        out_ref[...] = jnp.zeros_like(out_ref)

    for k in range(n):
        if k:
            up, down = gates[2 * k - 2 : 2 * k], gates[2 * (n - 1 - k) : 2 * (n - k)]
            below = up[0] if k == 1 else jnp.where(s_ref[n] > 0, up[0], up[1])
            above = down[1] if k == n - 1 else jnp.where(s_ref[n] > 0, down[1], down[0])
            gate = jnp.where(s_ref[n + k] > 0, below, above)
        else:
            gate = own_gate[...]
        hidden = held[k % group][0]
        for e in range(1, cores):
            hidden = jnp.where(s_ref[k] == e, held[k % group][e], hidden)
        high, low = split(hidden * gate.astype(F32))
        out_ref[k] += lax.dot_general(
            proj[...], high, ROWS_ROWS, preferred_element_type=F32
        ) + lax.dot_general(proj[...], low, ROWS_ROWS, preferred_element_type=F32)


def projected_first(n, cores, scalars, gate_act, proj_t, gates, hidden, after):
    part, hid = gates[0].shape
    half = part * CHUNKS
    step = block_of(hid, 512)
    flat = pl.BlockSpec((half, step), lambda i, s: (0, i))
    grid_spec = pltpu.PrefetchScalarGridSpec(
        num_scalar_prefetch=1,
        grid=(hid // step,),
        in_specs=[
            flat,
            pl.BlockSpec((R, step), lambda i, s: (0, i)),
        ]
        + [pl.BlockSpec((part, step), lambda i, s: (0, i))] * len(gates)
        + [pl.BlockSpec((cores, half, step), lambda i, s: (0, 0, i))] * len(hidden)
        + [ANYWHERE],
        out_specs=pl.BlockSpec((n, R, half), lambda i, s: (0, 0, 0)),
    )

    def kernel(*refs):
        first_kernel(n, cores, *refs)

    return pl.pallas_call(
        kernel,
        grid_spec=grid_spec,
        out_shape=jax.ShapeDtypeStruct((n, R, half), F32),
        compiler_params=pltpu.CompilerParams(vmem_limit_bytes=FIRST_LIMIT << 20),
        cost_estimate=cost(16),
        name="projected_first",
    )(scalars, gate_act, proj_t, *gates, *hidden, after)


def inputs_kernel(x_ref, proj_ref, after_ref, out_ref):
    del after_ref
    out_ref[...] = jnp.dot(x_ref[...], proj_ref[...], preferred_element_type=F32)


def projected_inputs(inputs, proj_in, after):
    whole = pl.BlockSpec(memory_space=pltpu.VMEM)
    return pl.pallas_call(
        inputs_kernel,
        in_specs=[whole, whole, ANYWHERE],
        out_specs=whole,
        out_shape=jax.ShapeDtypeStruct((inputs.shape[0], R), F32),
        compiler_params=pltpu.CompilerParams(vmem_limit_bytes=12 << 20),
        cost_estimate=cost(1),
        name="projected_inputs",
    )(inputs, proj_in, after)


def local(grad_out, inputs, gate_act, w_down, proj_in, proj_out, queries, example_of):
    n = lax.axis_size("blk")
    cores = lax.axis_size("sub")
    n_f = lax.axis_size("fsdp")
    z, x, core = lax.axis_index("blk"), lax.axis_index("fsdp"), lax.axis_index("sub")
    tok = grad_out.shape[0]
    hid, dblk = w_down.shape
    group = n // cores
    half = tok // 2

    def features(p):
        part = tok // n_f
        mine = lax.dynamic_slice(grad_out, (x * part, ((z + p) % group) * dblk), (part, dblk))
        route = []
        for zs in range(n):
            for cs in range(cores):
                zd = cs * group + (zs + p) % group
                route.append((zs * cores + cs, zd * cores + zs // group))
        return lax.ppermute(mine, ("blk", "sub"), route)

    def whole_of(got, after):
        parts = [got] + [shifted(got, "fsdp", e) for e in range(1, n_f)]
        return join(parts, x, after)

    def spread(whole):
        return [whole] + [shifted(whole, "sub", e) for e in range(1, cores)]

    def block_at(distance):
        return (core - ((z - distance) % n) // group) % cores

    def needed(step):
        return sorted({step % group, (n - step) % group})

    begin = needed(1)
    later = [p for p in range(group) if p not in begin]
    features_of = {p: features(p) for p in begin + later}
    part = half // CHUNKS
    even = x % 2 == 0
    came = []
    for c in range(CHUNKS):
        own = gate_act[c * part : (c + 1) * part]
        came.append([[line_right(own), line_left(own)]])
    waits = came[0][0] + [features_of[p] for p in later[:1]]
    whole = {p: whole_of(features_of[p], waits) for p in begin}
    spreads = {p: spread(whole[p]) for p in begin}
    last = example_of
    second, first = {}, {}
    for p in begin:
        last = hidden_grad(spreads[p], w_down, half, half, last)
        second[p] = (last, 0)
    for p in later:
        whole[p] = whole_of(features_of[p], [last])
    last, middle = whole[later[0]], None

    def counts(rightward):
        return jnp.where(rightward, z > 0, z < n - 1)

    for s in range(1, n):
        parts = [came] if s == n - 1 else [[stream] for stream in came]
        sent = []
        for c, streams in enumerate(parts):
            both = []
            for reverse in (False, True):
                rightward = even != reverse
                right, left = block_at(s), block_at(n - s)
                flags = [
                    counts(rightward),
                    jnp.where(rightward, z < s, z + s >= n),
                    jnp.logical_not(rightward),
                ]
                if s % group == (n - s) % group:
                    which, arrays = [jnp.where(rightward, right, left)] * 2, [second[s % group]]
                else:
                    which, arrays = [right, left], [second[s % group], second[(n - s) % group]]
                scalars = jnp.stack(which + [f.astype(jnp.int32) for f in flags])
                if s == 1:
                    got = [block for stream in streams for block in stream[-1]]
                else:
                    got = [stream[-1][int(reverse)] for stream in streams]
                rows_at = [start + c * part * len(streams) for _, start in arrays]
                arrays = [array for array, _ in arrays]
                last = payload(scalars, got, len(streams), arrays, rows_at, last)
                both.append(onward(last, reverse))
            sent.append(both)
        if s < n - 1:
            for stream, both in zip(came, sent, strict=True):
                stream.append(both)
        if s == n - 2:
            middle = last
        for p in needed(s + 1):
            if p not in second:
                spreads[p] = spread(whole[p])
                first[p] = last = hidden_grad(spreads[p], w_down, 0, tok, last)
                second[p] = (last, half)
        if s == n - 2:
            for p in begin:
                first[p] = last = hidden_grad(spreads[p], w_down, 0, half, last)

    width = R * R // cores
    own_q = block_copy(queries[0], 0 * z, 0 * z, queries.shape[1:], middle)
    own_q = own_q.reshape(cores, -1, width)
    got_q = [lax.dynamic_index_in_dim(own_q, core, 0, keepdims=False)]
    for e in range(1, cores):
        got_q.append(
            shifted(lax.dynamic_index_in_dim(own_q, (core + e) % cores, 0, keepdims=False), "sub", e)
        )
    own_q = jnp.concatenate([lax.select_n((core - i) % cores, *got_q) for i in range(cores)], axis=1)
    n_q = own_q.shape[0]
    flat_q = own_q.astype(F32).reshape(-1, half)

    gates = [came[c][s][d] for s in range(n - 1) for d in (0, 1) for c in range(CHUNKS)]
    scalars = [block_at(k) for k in range(n)] + [even] + [z >= k for k in range(1, n)]
    scalars = jnp.stack([f.astype(jnp.int32) for f in scalars])
    ups = projected_first(
        n,
        cores,
        scalars,
        gate_act,
        proj_out.T,
        gates,
        [first[p] for p in range(group)],
        last,
    )
    up_first = ups[0]
    got_q = [flat_q]
    for k in range(1, n):
        got = shifted(jnp.concatenate([ups[k], flat_q]), "blk", -k)
        up_first = up_first + got[:R]
        got_q.append(got[R:])
    all_q = jnp.stack([lax.select_n((i - z) % n, *got_q) for i in range(n)])
    all_q = all_q.reshape(n, n_q, R * R).astype(BF16)

    own_second = lax.dynamic_index_in_dim(second[0][0], block_at(0), 0, keepdims=False)[second[0][1] :]
    total = own_second + sum(
        jnp.where(counts(even != bool(d)), sent[0][d].astype(F32), 0.0) for d in (0, 1)
    )
    up_second = lax.dot_general(
        proj_out.astype(F32),
        total * gate_act[half:].astype(F32),
        (((0,), (1,)), ((), ())),
        precision=lax.Precision.HIGH,
        preferred_element_type=F32,
    )
    up_proj = summed(jnp.concatenate([up_first, up_second], axis=1), ("sub", "fsdp"))

    left_proj = summed(projected_inputs(inputs, proj_in, middle), ("sub", "fsdp"))
    onehot = (example_of[:, None] == jnp.arange(EX_DEV, dtype=jnp.int32)[None, :]).astype(F32)
    weighted = (onehot[:, :, None] * left_proj[:, None, :]).reshape(tok, EX_DEV * R)
    full_sketch = lax.dot_general(
        weighted, up_proj, (((0,), (1,)), ((), ())), precision=lax.Precision.HIGHEST
    )
    sketch = full_sketch.reshape(EX_DEV, R * R).astype(BF16)
    sketch_part = lax.dynamic_slice(sketch, (0, core * width), (EX_DEV, width))
    scores = lax.dot_general(
        sketch, all_q, (((1,), (2,)), ((), ())), preferred_element_type=F32
    )
    return sketch_part, scores


def solution(mesh):
    in_specs = (
        P(("groups", "blk"), "sub"),
        P(("groups", "blk"), ("fsdp", "sub")),
        P(("groups", "blk"), ("fsdp", "sub")),
        P(("fsdp", "sub"), "blk"),
        P(("fsdp", "sub"), None),
        P(("fsdp", "sub"), None),
        P(("groups", "blk"), "fsdp", "sub"),
        P(("groups", "blk")),
    )
    out_specs = (P(("groups", "blk"), "sub"), P(("groups", "blk"), None, ("fsdp", "sub")))
    return jax.shard_map(local, mesh=mesh, in_specs=in_specs, out_specs=out_specs, check_vma=False)
```

```python
import jax
import jax.numpy as jnp
from jax import lax
from jax.experimental import pallas as pl
from jax.experimental.pallas import tpu as pltpu
from jax.sharding import PartitionSpec as P

R = 64
EX_DEV = 8
LANES = 128
CHUNKS = 2
FIRST_LIMIT = 56
PAYLOAD_LIMIT = 12
F32 = jnp.float32
BF16 = jnp.bfloat16
ROWS_ROWS = (((1,), (1,)), ((), ()))
ANYWHERE = pl.BlockSpec(memory_space=pl.ANY)


def line_right(block):
    n = lax.axis_size("blk")
    return lax.ppermute(block, "blk", [(i, i + 1) for i in range(n - 1)])


def line_left(block):
    n = lax.axis_size("blk")
    return lax.ppermute(block, "blk", [(i + 1, i) for i in range(n - 1)])


def onward(block, reverse):
    n, n_f = lax.axis_size("blk"), lax.axis_size("fsdp")
    route = []
    for z in range(n):
        for x in range(n_f):
            to = z + (1 if (x % 2 == 0) != reverse else -1)
            route.append((z * n_f + x, to * n_f + x if 0 <= to < n else z * n_f + (x ^ 1)))
    return lax.ppermute(block, ("blk", "fsdp"), route)


def shifted(block, axis, distance):
    n = lax.axis_size(axis)
    return lax.ppermute(block, axis, [(i, (i + distance) % n) for i in range(n)])


def gathered(block, axis):
    n = lax.axis_size(axis)
    if n == 1:
        return block[None]
    here = lax.axis_index(axis)
    got = [block] + [shifted(block, axis, e) for e in range(1, n)]
    return jnp.stack([lax.select_n((here - i) % n, *got) for i in range(n)])


def summed(block, axes):
    for axis in axes:
        n = lax.axis_size(axis)
        step = 1
        while step < n:
            block = block + lax.ppermute(block, axis, [(i, i ^ step) for i in range(n)])
            step *= 2
    return block


def block_of(size, most):
    return max(b for b in range(LANES, most + 1, LANES) if size % b == 0)


def split(block):
    high = block.astype(BF16)
    return high, (block - high.astype(F32)).astype(BF16)


SHORT = pl.CostEstimate(flops=1000, bytes_accessed=1000, transcendentals=0)


def cost(microseconds):
    return pl.CostEstimate(
        flops=1000, bytes_accessed=3_690_000 * microseconds, transcendentals=0
    )


def stack_kernel(*refs):
    out_ref = refs[-1]
    for i, ref in enumerate(refs[:-2]):
        out_ref[i] = ref[...]


def hidden_grad(blocks, w_down, start, rows, after):
    depth = blocks[0].shape[1]
    stacked = pl.pallas_call(
        stack_kernel,
        grid=(1,),
        in_specs=[pl.BlockSpec((rows, depth), lambda i: (start // rows, 0))] * len(blocks)
        + [ANYWHERE],
        out_specs=pl.BlockSpec((len(blocks), rows, depth), lambda i: (0, 0, 0)),
        out_shape=jax.ShapeDtypeStruct((len(blocks), rows, depth), BF16),
        compiler_params=pltpu.CompilerParams(vmem_limit_bytes=16 << 20),
        cost_estimate=cost(1),
        name="stack",
    )(*blocks, after)
    out = lax.dot_general(
        stacked.reshape(-1, depth), w_down, ROWS_ROWS, preferred_element_type=F32
    )
    return out.reshape(len(blocks), rows, -1)


def join_kernel(n, s_ref, *refs):
    blocks, out_ref = refs[:n], refs[-1]
    rows = blocks[0].shape[0]
    for e, block in enumerate(blocks):
        start = pl.multiple_of(lax.rem(s_ref[0] + n - e, n) * rows, rows)
        out_ref[pl.ds(start, rows), :] = block[...]


def join(blocks, here, after):
    n = len(blocks)
    rows, depth = blocks[0].shape
    whole = pl.BlockSpec((rows, depth), lambda i, s: (0, 0))

    def kernel(*refs):
        join_kernel(n, *refs)

    return pl.pallas_call(
        kernel,
        grid_spec=pltpu.PrefetchScalarGridSpec(
            num_scalar_prefetch=1,
            grid=(1,),
            in_specs=[whole] * n + [ANYWHERE] * len(after),
            out_specs=pl.BlockSpec((n * rows, depth), lambda i, s: (0, 0)),
        ),
        out_shape=jax.ShapeDtypeStruct((n * rows, depth), BF16),
        compiler_params=pltpu.CompilerParams(vmem_limit_bytes=12 << 20),
        cost_estimate=SHORT,
        name="join",
    )(here.reshape(1), *blocks, *after)


def copy_kernel(s_ref, block_ref, after_ref, out_ref):
    del s_ref, after_ref
    out_ref[...] = block_ref[...]


def block_copy(array, row, column, shape, after):
    grid_spec = pltpu.PrefetchScalarGridSpec(
        num_scalar_prefetch=1,
        grid=(1,),
        in_specs=[pl.BlockSpec(shape, lambda i, s: (s[0], s[1])), ANYWHERE],
        out_specs=pl.BlockSpec(shape, lambda i, s: (0, 0)),
    )
    return pl.pallas_call(
        copy_kernel,
        grid_spec=grid_spec,
        out_shape=jax.ShapeDtypeStruct(shape, array.dtype),
        compiler_params=pltpu.CompilerParams(vmem_limit_bytes=12 << 20),
        cost_estimate=cost(1),
        name="block_copy",
    )(jnp.stack([row, column]).astype(jnp.int32), array, after)


def payload_kernel(n_got, n_mine, s_ref, *refs):
    got, mine, out_ref = refs[:n_got], refs[n_got : n_got + n_mine], refs[-1]
    rows = got[0].shape[0]
    each = n_got // (out_ref.shape[0] // rows)
    for c in range(n_got // each):
        at = pl.ds(c * rows, rows)
        term = mine[0][0, at, :]
        if n_mine == 2:
            term = jnp.where(s_ref[4] > 0, mine[1][0, at, :], term)
        came = got[c * each][...]
        if each == 2:
            came = jnp.where(s_ref[4] > 0, got[c * each + 1][...], came)
        came = jnp.where(s_ref[2] > 0, came.astype(F32), 0.0)
        out_ref[at, :] = (came + jnp.where(s_ref[3] > 0, term, 0.0)).astype(BF16)


def payload(scalars, got, parts, hidden, rows_at, *after):
    part, hid = got[0].shape
    rows = part * parts
    step = block_of(hid, 1792)
    grid_spec = pltpu.PrefetchScalarGridSpec(
        num_scalar_prefetch=1,
        grid=(hid // step,),
        in_specs=[pl.BlockSpec((part, step), lambda i, s: (0, i))] * len(got)
        + [
            pl.BlockSpec((1, rows, step), lambda i, s, j=j: (s[j], rows_at[j] // rows, i))
            for j in range(len(hidden))
        ]
        + [ANYWHERE] * len(after),
        out_specs=pl.BlockSpec((rows, step), lambda i, s: (0, i)),
    )

    def kernel(*refs):
        payload_kernel(len(got), len(hidden), *refs)

    return pl.pallas_call(
        kernel,
        grid_spec=grid_spec,
        out_shape=jax.ShapeDtypeStruct((rows, hid), BF16),
        compiler_params=pltpu.CompilerParams(vmem_limit_bytes=PAYLOAD_LIMIT << 20),
        cost_estimate=SHORT,
        name="payload",
    )(scalars, *got, *hidden, *after)


def first_kernel(n, cores, s_ref, own_gate, proj, *refs):
    group = n // cores
    held, out_ref = refs[-2 - group : -2], refs[-1]
    gates = [
        jnp.concatenate([ref[...] for ref in refs[i * CHUNKS : (i + 1) * CHUNKS]])
        for i in range(2 * n - 2)
    ]

    @pl.when(pl.program_id(0) == 0)
    def _():
        out_ref[...] = jnp.zeros_like(out_ref)

    for k in range(n):
        if k:
            up, down = gates[2 * k - 2 : 2 * k], gates[2 * (n - 1 - k) : 2 * (n - k)]
            below = up[0] if k == 1 else jnp.where(s_ref[n] > 0, up[0], up[1])
            above = down[1] if k == n - 1 else jnp.where(s_ref[n] > 0, down[1], down[0])
            gate = jnp.where(s_ref[n + k] > 0, below, above)
        else:
            gate = own_gate[...]
        hidden = held[k % group][0]
        for e in range(1, cores):
            hidden = jnp.where(s_ref[k] == e, held[k % group][e], hidden)
        high, low = split(hidden * gate.astype(F32))
        out_ref[k] += lax.dot_general(
            proj[...], high, ROWS_ROWS, preferred_element_type=F32
        ) + lax.dot_general(proj[...], low, ROWS_ROWS, preferred_element_type=F32)


def projected_first(n, cores, scalars, gate_act, proj_t, gates, hidden, after):
    part, hid = gates[0].shape
    half = part * CHUNKS
    step = block_of(hid, 512)
    flat = pl.BlockSpec((half, step), lambda i, s: (0, i))
    grid_spec = pltpu.PrefetchScalarGridSpec(
        num_scalar_prefetch=1,
        grid=(hid // step,),
        in_specs=[
            flat,
            pl.BlockSpec((R, step), lambda i, s: (0, i)),
        ]
        + [pl.BlockSpec((part, step), lambda i, s: (0, i))] * len(gates)
        + [pl.BlockSpec((cores, half, step), lambda i, s: (0, 0, i))] * len(hidden)
        + [ANYWHERE],
        out_specs=pl.BlockSpec((n, R, half), lambda i, s: (0, 0, 0)),
    )

    def kernel(*refs):
        first_kernel(n, cores, *refs)

    return pl.pallas_call(
        kernel,
        grid_spec=grid_spec,
        out_shape=jax.ShapeDtypeStruct((n, R, half), F32),
        compiler_params=pltpu.CompilerParams(vmem_limit_bytes=FIRST_LIMIT << 20),
        cost_estimate=cost(16),
        name="projected_first",
    )(scalars, gate_act, proj_t, *gates, *hidden, after)


def inputs_kernel(x_ref, proj_ref, after_ref, out_ref):
    del after_ref
    out_ref[...] = lax.dot_general(
        x_ref[...], proj_ref[...], ROWS_ROWS, preferred_element_type=F32
    )


def projected_inputs(inputs, proj_t, after):
    whole = pl.BlockSpec(memory_space=pltpu.VMEM)
    return pl.pallas_call(
        inputs_kernel,
        in_specs=[whole, whole, ANYWHERE],
        out_specs=whole,
        out_shape=jax.ShapeDtypeStruct((inputs.shape[0], R), F32),
        compiler_params=pltpu.CompilerParams(vmem_limit_bytes=12 << 20),
        cost_estimate=cost(1),
        name="projected_inputs",
    )(inputs, proj_t, after)


def local(grad_out, inputs, gate_act, w_down, proj_in, proj_out, queries, example_of):
    n = lax.axis_size("blk")
    cores = lax.axis_size("sub")
    n_f = lax.axis_size("fsdp")
    z, x, core = lax.axis_index("blk"), lax.axis_index("fsdp"), lax.axis_index("sub")
    tok = grad_out.shape[0]
    hid, dblk = w_down.shape
    group = n // cores
    half = tok // 2

    def features(p):
        part = tok // n_f
        mine = lax.dynamic_slice(grad_out, (x * part, ((z + p) % group) * dblk), (part, dblk))
        route = []
        for zs in range(n):
            for cs in range(cores):
                zd = cs * group + (zs + p) % group
                route.append((zs * cores + cs, zd * cores + zs // group))
        return lax.ppermute(mine, ("blk", "sub"), route)

    def whole_of(got, after):
        parts = [got] + [shifted(got, "fsdp", e) for e in range(1, n_f)]
        return join(parts, x, after)

    def spread(whole):
        return [whole] + [shifted(whole, "sub", e) for e in range(1, cores)]

    def block_at(distance):
        return (core - ((z - distance) % n) // group) % cores

    def needed(step):
        return sorted({step % group, (n - step) % group})

    begin = needed(1)
    later = [p for p in range(group) if p not in begin]
    features_of = {p: features(p) for p in begin + later}
    part = half // CHUNKS
    even = x % 2 == 0
    came = []
    for c in range(CHUNKS):
        own = gate_act[c * part : (c + 1) * part]
        came.append([[line_right(own), line_left(own)]])
    waits = came[0][0] + [features_of[p] for p in later[:1]]
    whole = {p: whole_of(features_of[p], waits) for p in begin}
    spreads = {p: spread(whole[p]) for p in begin}
    last = example_of
    second, first = {}, {}
    for p in begin:
        last = hidden_grad(spreads[p], w_down, half, half, last)
        second[p] = (last, 0)
    for p in later:
        whole[p] = whole_of(features_of[p], [last] + came[-1][0])
    last, all_q = [whole[later[0]]], None

    width = R * R // cores

    def all_queries(after):
        own_q = block_copy(queries[0], 0 * z, 0 * z, queries.shape[1:], after)
        own_q = own_q.reshape(cores, -1, width)
        got_q = [lax.dynamic_index_in_dim(own_q, core, 0, keepdims=False)]
        for e in range(1, cores):
            got_q.append(
                shifted(lax.dynamic_index_in_dim(own_q, (core + e) % cores, 0, keepdims=False), "sub", e)
            )
        own_q = jnp.concatenate([lax.select_n((core - i) % cores, *got_q) for i in range(cores)], axis=1)
        return gathered(own_q, "blk")

    def counts(rightward):
        return jnp.where(rightward, z > 0, z < n - 1)

    for s in range(1, n):
        parts = [came] if s == n - 1 else [[stream] for stream in came]
        sent = []
        for c, streams in enumerate(parts):
            both = []
            for reverse in (False, True):
                rightward = even != reverse
                right, left = block_at(s), block_at(n - s)
                flags = [
                    counts(rightward),
                    jnp.where(rightward, z < s, z + s >= n),
                    jnp.logical_not(rightward),
                ]
                if s % group == (n - s) % group:
                    which, arrays = [jnp.where(rightward, right, left)] * 2, [second[s % group]]
                else:
                    which, arrays = [right, left], [second[s % group], second[(n - s) % group]]
                scalars = jnp.stack(which + [f.astype(jnp.int32) for f in flags])
                if s == 1:
                    got = [block for stream in streams for block in stream[-1]]
                else:
                    got = [stream[-1][int(reverse)] for stream in streams]
                rows_at = [start + c * part * len(streams) for _, start in arrays]
                arrays = [array for array, _ in arrays]
                last = payload(scalars, got, len(streams), arrays, rows_at, *last)
                last = [last]
                both.append(onward(last[0], reverse))
            sent.append(both)
        if s < n - 1:
            for stream, both in zip(came, sent, strict=True):
                stream.append(both)
        if s == n - 2:
            all_q = all_queries(last[0])
        for p in needed(s + 1):
            if p not in second:
                spreads[p] = spread(whole[p])
                first[p] = hidden_grad(spreads[p], w_down, 0, tok, last[0])
                last, second[p] = [first[p]], (first[p], half)
        if s == n - 2:
            for p in begin:
                first[p] = hidden_grad(spreads[p], w_down, 0, half, last[0])
                last = [first[p]]

    gates = [came[c][s][d] for s in range(n - 1) for d in (0, 1) for c in range(CHUNKS)]
    scalars = [block_at(k) for k in range(n)] + [even] + [z >= k for k in range(1, n)]
    scalars = jnp.stack([f.astype(jnp.int32) for f in scalars])
    ups = projected_first(
        n,
        cores,
        scalars,
        gate_act,
        proj_out.T,
        gates,
        [first[p] for p in range(group)],
        last[0],
    )
    up_first = ups[0]
    for k in range(1, n):
        up_first = up_first + shifted(ups[k], "blk", -k)

    own_second = lax.dynamic_index_in_dim(second[0][0], block_at(0), 0, keepdims=False)[second[0][1] :]
    total = own_second + sum(
        jnp.where(counts(even != bool(d)), sent[0][d].astype(F32), 0.0) for d in (0, 1)
    )
    up_second = lax.dot_general(
        proj_out.astype(F32),
        total * gate_act[half:].astype(F32),
        (((0,), (1,)), ((), ())),
        precision=lax.Precision.HIGH,
        preferred_element_type=F32,
    )
    up_proj = summed(jnp.concatenate([up_first, up_second], axis=1), ("sub", "fsdp"))

    left_proj = summed(projected_inputs(inputs, proj_in.T, ups), ("sub", "fsdp"))
    onehot = (example_of[:, None] == jnp.arange(EX_DEV, dtype=jnp.int32)[None, :]).astype(F32)
    weighted = (onehot[:, :, None] * left_proj[:, None, :]).reshape(tok, EX_DEV * R)
    full_sketch = lax.dot_general(
        weighted, up_proj, (((0,), (1,)), ((), ())), precision=lax.Precision.HIGHEST
    )
    sketch = full_sketch.reshape(EX_DEV, R * R).astype(BF16)
    sketch_part = lax.dynamic_slice(sketch, (0, core * width), (EX_DEV, width))
    scores = lax.dot_general(
        sketch, all_q, (((1,), (2,)), ((), ())), preferred_element_type=F32
    )
    return sketch_part, scores


def solution(mesh):
    in_specs = (
        P(("groups", "blk"), "sub"),
        P(("groups", "blk"), ("fsdp", "sub")),
        P(("groups", "blk"), ("fsdp", "sub")),
        P(("fsdp", "sub"), "blk"),
        P(("fsdp", "sub"), None),
        P(("fsdp", "sub"), None),
        P(("groups", "blk"), "fsdp", "sub"),
        P(("groups", "blk")),
    )
    out_specs = (P(("groups", "blk"), "sub"), P(("groups", "blk"), None, ("fsdp", "sub")))
    return jax.shard_map(local, mesh=mesh, in_specs=in_specs, out_specs=out_specs, check_vma=False)
```

```python
import jax
import jax.numpy as jnp
from jax import lax
from jax.experimental import pallas as pl
from jax.experimental.pallas import tpu as pltpu
from jax.sharding import PartitionSpec as P

R = 64
EX_DEV = 8
LANES = 128
CHUNKS = 2
FIRST_LIMIT = 56
PAYLOAD_LIMIT = 12
F32 = jnp.float32
BF16 = jnp.bfloat16
ROWS_ROWS = (((1,), (1,)), ((), ()))
ANYWHERE = pl.BlockSpec(memory_space=pl.ANY)


def line_right(block):
    n = lax.axis_size("blk")
    return lax.ppermute(block, "blk", [(i, i + 1) for i in range(n - 1)])


def line_left(block):
    n = lax.axis_size("blk")
    return lax.ppermute(block, "blk", [(i + 1, i) for i in range(n - 1)])


def onward(block, reverse):
    n, n_f = lax.axis_size("blk"), lax.axis_size("fsdp")
    route = []
    for z in range(n):
        for x in range(n_f):
            to = z + (1 if (x % 2 == 0) != reverse else -1)
            route.append((z * n_f + x, to * n_f + x if 0 <= to < n else z * n_f + (x ^ 1)))
    return lax.ppermute(block, ("blk", "fsdp"), route)


def shifted(block, axis, distance):
    n = lax.axis_size(axis)
    return lax.ppermute(block, axis, [(i, (i + distance) % n) for i in range(n)])


def gathered(block, axis):
    n = lax.axis_size(axis)
    if n == 1:
        return block[None]
    here = lax.axis_index(axis)
    got = [block] + [shifted(block, axis, e) for e in range(1, n)]
    return jnp.stack([lax.select_n((here - i) % n, *got) for i in range(n)])


def summed(block, axes):
    for axis in axes:
        n = lax.axis_size(axis)
        step = 1
        while step < n:
            block = block + lax.ppermute(block, axis, [(i, i ^ step) for i in range(n)])
            step *= 2
    return block


def block_of(size, most):
    return max(b for b in range(LANES, most + 1, LANES) if size % b == 0)


def split(block):
    high = block.astype(BF16)
    return high, (block - high.astype(F32)).astype(BF16)


SHORT = pl.CostEstimate(flops=1000, bytes_accessed=1000, transcendentals=0)


def cost(microseconds):
    return pl.CostEstimate(
        flops=1000, bytes_accessed=3_690_000 * microseconds, transcendentals=0
    )


def stack_kernel(*refs):
    out_ref = refs[-1]
    for i, ref in enumerate(refs[:-2]):
        out_ref[i] = ref[...]


def hidden_grad(blocks, w_down, start, rows, after):
    depth = blocks[0].shape[1]
    stacked = pl.pallas_call(
        stack_kernel,
        grid=(1,),
        in_specs=[pl.BlockSpec((rows, depth), lambda i: (start // rows, 0))] * len(blocks)
        + [ANYWHERE],
        out_specs=pl.BlockSpec((len(blocks), rows, depth), lambda i: (0, 0, 0)),
        out_shape=jax.ShapeDtypeStruct((len(blocks), rows, depth), BF16),
        compiler_params=pltpu.CompilerParams(vmem_limit_bytes=16 << 20),
        cost_estimate=cost(1),
        name="stack",
    )(*blocks, after)
    out = lax.dot_general(
        stacked.reshape(-1, depth), w_down, ROWS_ROWS, preferred_element_type=F32
    )
    return out.reshape(len(blocks), rows, -1)


def join_kernel(n, s_ref, *refs):
    blocks, out_ref = refs[:n], refs[-1]
    rows = blocks[0].shape[0]
    for e, block in enumerate(blocks):
        start = pl.multiple_of(lax.rem(s_ref[0] + n - e, n) * rows, rows)
        out_ref[pl.ds(start, rows), :] = block[...]


def join(blocks, here, after):
    n = len(blocks)
    rows, depth = blocks[0].shape
    whole = pl.BlockSpec((rows, depth), lambda i, s: (0, 0))

    def kernel(*refs):
        join_kernel(n, *refs)

    return pl.pallas_call(
        kernel,
        grid_spec=pltpu.PrefetchScalarGridSpec(
            num_scalar_prefetch=1,
            grid=(1,),
            in_specs=[whole] * n + [ANYWHERE] * len(after),
            out_specs=pl.BlockSpec((n * rows, depth), lambda i, s: (0, 0)),
        ),
        out_shape=jax.ShapeDtypeStruct((n * rows, depth), BF16),
        compiler_params=pltpu.CompilerParams(vmem_limit_bytes=12 << 20),
        cost_estimate=SHORT,
        name="join",
    )(here.reshape(1), *blocks, *after)


def copy_kernel(s_ref, block_ref, after_ref, out_ref):
    del s_ref, after_ref
    out_ref[...] = block_ref[...]


def block_copy(array, row, column, shape, after):
    grid_spec = pltpu.PrefetchScalarGridSpec(
        num_scalar_prefetch=1,
        grid=(1,),
        in_specs=[pl.BlockSpec(shape, lambda i, s: (s[0], s[1])), ANYWHERE],
        out_specs=pl.BlockSpec(shape, lambda i, s: (0, 0)),
    )
    return pl.pallas_call(
        copy_kernel,
        grid_spec=grid_spec,
        out_shape=jax.ShapeDtypeStruct(shape, array.dtype),
        compiler_params=pltpu.CompilerParams(vmem_limit_bytes=12 << 20),
        cost_estimate=cost(1),
        name="block_copy",
    )(jnp.stack([row, column]).astype(jnp.int32), array, after)


def payload_kernel(n_got, n_mine, s_ref, *refs):
    got, mine, out_ref = refs[:n_got], refs[n_got : n_got + n_mine], refs[-1]
    rows = got[0].shape[0]
    each = n_got // (out_ref.shape[0] // rows)
    for c in range(n_got // each):
        at = pl.ds(c * rows, rows)
        term = mine[0][0, at, :]
        if n_mine == 2:
            term = jnp.where(s_ref[4] > 0, mine[1][0, at, :], term)
        came = got[c * each][...]
        if each == 2:
            came = jnp.where(s_ref[4] > 0, got[c * each + 1][...], came)
        came = jnp.where(s_ref[2] > 0, came.astype(F32), 0.0)
        out_ref[at, :] = (came + jnp.where(s_ref[3] > 0, term, 0.0)).astype(BF16)


def payload(scalars, got, parts, hidden, rows_at, *after):
    part, hid = got[0].shape
    rows = part * parts
    step = block_of(hid, 1792)
    grid_spec = pltpu.PrefetchScalarGridSpec(
        num_scalar_prefetch=1,
        grid=(hid // step,),
        in_specs=[pl.BlockSpec((part, step), lambda i, s: (0, i))] * len(got)
        + [
            pl.BlockSpec((1, rows, step), lambda i, s, j=j: (s[j], rows_at[j] // rows, i))
            for j in range(len(hidden))
        ]
        + [ANYWHERE] * len(after),
        out_specs=pl.BlockSpec((rows, step), lambda i, s: (0, i)),
    )

    def kernel(*refs):
        payload_kernel(len(got), len(hidden), *refs)

    return pl.pallas_call(
        kernel,
        grid_spec=grid_spec,
        out_shape=jax.ShapeDtypeStruct((rows, hid), BF16),
        compiler_params=pltpu.CompilerParams(vmem_limit_bytes=PAYLOAD_LIMIT << 20),
        cost_estimate=SHORT,
        name="payload",
    )(scalars, *got, *hidden, *after)


def first_kernel(n, cores, s_ref, own_gate, proj, *refs):
    group = n // cores
    held, out_ref = refs[-2 - group : -2], refs[-1]
    gates = [
        jnp.concatenate([ref[...] for ref in refs[i * CHUNKS : (i + 1) * CHUNKS]])
        for i in range(2 * n - 2)
    ]

    @pl.when(pl.program_id(0) == 0)
    def _():
        out_ref[...] = jnp.zeros_like(out_ref)

    for k in range(n):
        if k:
            up, down = gates[2 * k - 2 : 2 * k], gates[2 * (n - 1 - k) : 2 * (n - k)]
            below = up[0] if k == 1 else jnp.where(s_ref[n] > 0, up[0], up[1])
            above = down[1] if k == n - 1 else jnp.where(s_ref[n] > 0, down[1], down[0])
            gate = jnp.where(s_ref[n + k] > 0, below, above)
        else:
            gate = own_gate[...]
        hidden = held[k % group][0]
        for e in range(1, cores):
            hidden = jnp.where(s_ref[k] == e, held[k % group][e], hidden)
        high, low = split(hidden * gate.astype(F32))
        out_ref[k] += lax.dot_general(
            proj[...], high, ROWS_ROWS, preferred_element_type=F32
        ) + lax.dot_general(proj[...], low, ROWS_ROWS, preferred_element_type=F32)


def projected_first(n, cores, scalars, gate_act, proj_t, gates, hidden, after):
    part, hid = gates[0].shape
    half = part * CHUNKS
    step = block_of(hid, 512)
    flat = pl.BlockSpec((half, step), lambda i, s: (0, i))
    grid_spec = pltpu.PrefetchScalarGridSpec(
        num_scalar_prefetch=1,
        grid=(hid // step,),
        in_specs=[
            flat,
            pl.BlockSpec((R, step), lambda i, s: (0, i)),
        ]
        + [pl.BlockSpec((part, step), lambda i, s: (0, i))] * len(gates)
        + [pl.BlockSpec((cores, half, step), lambda i, s: (0, 0, i))] * len(hidden)
        + [ANYWHERE],
        out_specs=pl.BlockSpec((n, R, half), lambda i, s: (0, 0, 0)),
    )

    def kernel(*refs):
        first_kernel(n, cores, *refs)

    return pl.pallas_call(
        kernel,
        grid_spec=grid_spec,
        out_shape=jax.ShapeDtypeStruct((n, R, half), F32),
        compiler_params=pltpu.CompilerParams(vmem_limit_bytes=FIRST_LIMIT << 20),
        cost_estimate=cost(16),
        name="projected_first",
    )(scalars, gate_act, proj_t, *gates, *hidden, after)


def inputs_kernel(x_ref, proj_ref, after_ref, out_ref):
    del after_ref
    out_ref[...] = lax.dot_general(
        x_ref[...], proj_ref[...], ROWS_ROWS, preferred_element_type=F32
    )


def projected_inputs(inputs, proj_t, after):
    whole = pl.BlockSpec(memory_space=pltpu.VMEM)
    return pl.pallas_call(
        inputs_kernel,
        in_specs=[whole, whole, ANYWHERE],
        out_specs=whole,
        out_shape=jax.ShapeDtypeStruct((inputs.shape[0], R), F32),
        compiler_params=pltpu.CompilerParams(vmem_limit_bytes=12 << 20),
        cost_estimate=cost(1),
        name="projected_inputs",
    )(inputs, proj_t, after)


def local(grad_out, inputs, gate_act, w_down, proj_in, proj_out, queries, example_of):
    n = lax.axis_size("blk")
    cores = lax.axis_size("sub")
    n_f = lax.axis_size("fsdp")
    z, x, core = lax.axis_index("blk"), lax.axis_index("fsdp"), lax.axis_index("sub")
    tok = grad_out.shape[0]
    hid, dblk = w_down.shape
    group = n // cores
    half = tok // 2

    def features(p):
        part = tok // n_f
        mine = lax.dynamic_slice(grad_out, (x * part, ((z + p) % group) * dblk), (part, dblk))
        route = []
        for zs in range(n):
            for cs in range(cores):
                zd = cs * group + (zs + p) % group
                route.append((zs * cores + cs, zd * cores + zs // group))
        return lax.ppermute(mine, ("blk", "sub"), route)

    def whole_of(got, after):
        parts = [got] + [shifted(got, "fsdp", e) for e in range(1, n_f)]
        return join(parts, x, after)

    def spread(whole):
        return [whole] + [shifted(whole, "sub", e) for e in range(1, cores)]

    def block_at(distance):
        return (core - ((z - distance) % n) // group) % cores

    def needed(step):
        return sorted({step % group, (n - step) % group})

    begin = needed(1)
    later = [p for p in range(group) if p not in begin]
    features_of = {p: features(p) for p in begin + later}
    part = half // CHUNKS
    even = x % 2 == 0
    came = []
    for c in range(CHUNKS):
        own = gate_act[c * part : (c + 1) * part]
        came.append([[line_right(own), line_left(own)]])
    waits = came[0][0] + [features_of[p] for p in later[:1]]
    whole = {p: whole_of(features_of[p], waits) for p in begin}
    spreads = {p: spread(whole[p]) for p in begin}
    last = example_of
    second, first = {}, {}
    for p in begin:
        last = hidden_grad(spreads[p], w_down, half, half, last)
        second[p] = (last, 0)
    last, all_q = list(came[-1][0]), None

    width = R * R // cores

    def all_queries(after):
        own_q = block_copy(queries[0], 0 * z, 0 * z, queries.shape[1:], after)
        own_q = own_q.reshape(cores, -1, width)
        got_q = [lax.dynamic_index_in_dim(own_q, core, 0, keepdims=False)]
        for e in range(1, cores):
            got_q.append(
                shifted(lax.dynamic_index_in_dim(own_q, (core + e) % cores, 0, keepdims=False), "sub", e)
            )
        own_q = jnp.concatenate([lax.select_n((core - i) % cores, *got_q) for i in range(cores)], axis=1)
        return gathered(own_q, "blk")

    def counts(rightward):
        return jnp.where(rightward, z > 0, z < n - 1)

    for s in range(1, n):
        parts = [came] if s == n - 1 else [[stream] for stream in came]
        sent = []
        for c, streams in enumerate(parts):
            both = []
            for reverse in (False, True):
                rightward = even != reverse
                right, left = block_at(s), block_at(n - s)
                flags = [
                    counts(rightward),
                    jnp.where(rightward, z < s, z + s >= n),
                    jnp.logical_not(rightward),
                ]
                if s % group == (n - s) % group:
                    which, arrays = [jnp.where(rightward, right, left)] * 2, [second[s % group]]
                else:
                    which, arrays = [right, left], [second[s % group], second[(n - s) % group]]
                scalars = jnp.stack(which + [f.astype(jnp.int32) for f in flags])
                if s == 1:
                    got = [block for stream in streams for block in stream[-1]]
                else:
                    got = [stream[-1][int(reverse)] for stream in streams]
                rows_at = [start + c * part * len(streams) for _, start in arrays]
                arrays = [array for array, _ in arrays]
                if s == 1 and not reverse and c == len(parts) - 1:
                    for p in later:
                        whole[p] = whole_of(features_of[p], last)
                    last = last + [whole[later[0]]]
                last = payload(scalars, got, len(streams), arrays, rows_at, *last)
                last = [last]
                both.append(onward(last[0], reverse))
            sent.append(both)
        if s < n - 1:
            for stream, both in zip(came, sent, strict=True):
                stream.append(both)
        if s == n - 2:
            all_q = all_queries(last[0])
        for p in needed(s + 1):
            if p not in second:
                spreads[p] = spread(whole[p])
                first[p] = hidden_grad(spreads[p], w_down, 0, tok, last[0])
                last, second[p] = [first[p]], (first[p], half)
        if s == n - 2:
            for p in begin:
                first[p] = hidden_grad(spreads[p], w_down, 0, half, last[0])
                last = [first[p]]

    gates = [came[c][s][d] for s in range(n - 1) for d in (0, 1) for c in range(CHUNKS)]
    scalars = [block_at(k) for k in range(n)] + [even] + [z >= k for k in range(1, n)]
    scalars = jnp.stack([f.astype(jnp.int32) for f in scalars])
    ups = projected_first(
        n,
        cores,
        scalars,
        gate_act,
        proj_out.T,
        gates,
        [first[p] for p in range(group)],
        last[0],
    )
    up_first = ups[0]
    for k in range(1, n):
        up_first = up_first + shifted(ups[k], "blk", -k)

    own_second = lax.dynamic_index_in_dim(second[0][0], block_at(0), 0, keepdims=False)[second[0][1] :]
    total = own_second + sum(
        jnp.where(counts(even != bool(d)), sent[0][d].astype(F32), 0.0) for d in (0, 1)
    )
    up_second = lax.dot_general(
        proj_out.astype(F32),
        total * gate_act[half:].astype(F32),
        (((0,), (1,)), ((), ())),
        precision=lax.Precision.HIGH,
        preferred_element_type=F32,
    )
    up_proj = summed(jnp.concatenate([up_first, up_second], axis=1), ("sub", "fsdp"))

    left_proj = summed(projected_inputs(inputs, proj_in.T, ups), ("sub", "fsdp"))
    onehot = (example_of[:, None] == jnp.arange(EX_DEV, dtype=jnp.int32)[None, :]).astype(F32)
    weighted = (onehot[:, :, None] * left_proj[:, None, :]).reshape(tok, EX_DEV * R)
    full_sketch = lax.dot_general(
        weighted, up_proj, (((0,), (1,)), ((), ())), precision=lax.Precision.HIGHEST
    )
    sketch = full_sketch.reshape(EX_DEV, R * R).astype(BF16)
    sketch_part = lax.dynamic_slice(sketch, (0, core * width), (EX_DEV, width))
    scores = lax.dot_general(
        sketch, all_q, (((1,), (2,)), ((), ())), preferred_element_type=F32
    )
    return sketch_part, scores


def solution(mesh):
    in_specs = (
        P(("groups", "blk"), "sub"),
        P(("groups", "blk"), ("fsdp", "sub")),
        P(("groups", "blk"), ("fsdp", "sub")),
        P(("fsdp", "sub"), "blk"),
        P(("fsdp", "sub"), None),
        P(("fsdp", "sub"), None),
        P(("groups", "blk"), "fsdp", "sub"),
        P(("groups", "blk")),
    )
    out_specs = (P(("groups", "blk"), "sub"), P(("groups", "blk"), None, ("fsdp", "sub")))
    return jax.shard_map(local, mesh=mesh, in_specs=in_specs, out_specs=out_specs, check_vma=False)
```

```python
import jax
import jax.numpy as jnp
from jax import lax
from jax.experimental import pallas as pl
from jax.experimental.pallas import tpu as pltpu
from jax.sharding import PartitionSpec as P

R = 64
EX_DEV = 8
LANES = 128
CHUNKS = 2
FIRST_LIMIT = 56
PAYLOAD_LIMIT = 12
F32 = jnp.float32
BF16 = jnp.bfloat16
ROWS_ROWS = (((1,), (1,)), ((), ()))
ANYWHERE = pl.BlockSpec(memory_space=pl.ANY)


def line_right(block):
    n = lax.axis_size("blk")
    return lax.ppermute(block, "blk", [(i, i + 1) for i in range(n - 1)])


def line_left(block):
    n = lax.axis_size("blk")
    return lax.ppermute(block, "blk", [(i + 1, i) for i in range(n - 1)])


def onward(block, reverse):
    n, n_f = lax.axis_size("blk"), lax.axis_size("fsdp")
    route = []
    for z in range(n):
        for x in range(n_f):
            to = z + (1 if (x % 2 == 0) != reverse else -1)
            route.append((z * n_f + x, to * n_f + x if 0 <= to < n else z * n_f + (x ^ 1)))
    return lax.ppermute(block, ("blk", "fsdp"), route)


def shifted(block, axis, distance):
    n = lax.axis_size(axis)
    return lax.ppermute(block, axis, [(i, (i + distance) % n) for i in range(n)])


def gathered(block, axis):
    n = lax.axis_size(axis)
    if n == 1:
        return block[None]
    here = lax.axis_index(axis)
    got = [block] + [shifted(block, axis, e) for e in range(1, n)]
    return jnp.stack([lax.select_n((here - i) % n, *got) for i in range(n)])


def summed(block, axes):
    for axis in axes:
        n = lax.axis_size(axis)
        step = 1
        while step < n:
            block = block + lax.ppermute(block, axis, [(i, i ^ step) for i in range(n)])
            step *= 2
    return block


def block_of(size, most):
    return max(b for b in range(LANES, most + 1, LANES) if size % b == 0)


def split(block):
    high = block.astype(BF16)
    return high, (block - high.astype(F32)).astype(BF16)


SHORT = pl.CostEstimate(flops=1000, bytes_accessed=1000, transcendentals=0)


def cost(microseconds):
    return pl.CostEstimate(
        flops=1000, bytes_accessed=3_690_000 * microseconds, transcendentals=0
    )


def stack_kernel(*refs):
    out_ref = refs[-1]
    for i, ref in enumerate(refs[:-2]):
        out_ref[i] = ref[...]


def hidden_grad(blocks, w_down, start, rows, after):
    depth = blocks[0].shape[1]
    stacked = pl.pallas_call(
        stack_kernel,
        grid=(1,),
        in_specs=[pl.BlockSpec((rows, depth), lambda i: (start // rows, 0))] * len(blocks)
        + [ANYWHERE],
        out_specs=pl.BlockSpec((len(blocks), rows, depth), lambda i: (0, 0, 0)),
        out_shape=jax.ShapeDtypeStruct((len(blocks), rows, depth), BF16),
        compiler_params=pltpu.CompilerParams(vmem_limit_bytes=16 << 20),
        cost_estimate=cost(1),
        name="stack",
    )(*blocks, after)
    out = lax.dot_general(
        stacked.reshape(-1, depth), w_down, ROWS_ROWS, preferred_element_type=F32
    )
    return out.reshape(len(blocks), rows, -1)


def join_kernel(n, s_ref, *refs):
    blocks, out_ref = refs[:n], refs[-1]
    rows = blocks[0].shape[0]
    for e, block in enumerate(blocks):
        start = pl.multiple_of(lax.rem(s_ref[0] + n - e, n) * rows, rows)
        out_ref[pl.ds(start, rows), :] = block[...]


def join(blocks, here, after):
    n = len(blocks)
    rows, depth = blocks[0].shape
    whole = pl.BlockSpec((rows, depth), lambda i, s: (0, 0))

    def kernel(*refs):
        join_kernel(n, *refs)

    return pl.pallas_call(
        kernel,
        grid_spec=pltpu.PrefetchScalarGridSpec(
            num_scalar_prefetch=1,
            grid=(1,),
            in_specs=[whole] * n + [ANYWHERE] * len(after),
            out_specs=pl.BlockSpec((n * rows, depth), lambda i, s: (0, 0)),
        ),
        out_shape=jax.ShapeDtypeStruct((n * rows, depth), BF16),
        compiler_params=pltpu.CompilerParams(vmem_limit_bytes=12 << 20),
        cost_estimate=SHORT,
        name="join",
    )(here.reshape(1), *blocks, *after)


def copy_kernel(s_ref, block_ref, after_ref, out_ref):
    del s_ref, after_ref
    out_ref[...] = block_ref[...]


def block_copy(array, row, column, shape, after):
    grid_spec = pltpu.PrefetchScalarGridSpec(
        num_scalar_prefetch=1,
        grid=(1,),
        in_specs=[pl.BlockSpec(shape, lambda i, s: (s[0], s[1])), ANYWHERE],
        out_specs=pl.BlockSpec(shape, lambda i, s: (0, 0)),
    )
    return pl.pallas_call(
        copy_kernel,
        grid_spec=grid_spec,
        out_shape=jax.ShapeDtypeStruct(shape, array.dtype),
        compiler_params=pltpu.CompilerParams(vmem_limit_bytes=12 << 20),
        cost_estimate=cost(1),
        name="block_copy",
    )(jnp.stack([row, column]).astype(jnp.int32), array, after)


def payload_kernel(n_got, n_mine, s_ref, *refs):
    got, mine, out_ref = refs[:n_got], refs[n_got : n_got + n_mine], refs[-1]
    rows = got[0].shape[0]
    each = n_got // (out_ref.shape[0] // rows)
    for c in range(n_got // each):
        at = pl.ds(c * rows, rows)
        term = mine[0][0, at, :]
        if n_mine == 2:
            term = jnp.where(s_ref[4] > 0, mine[1][0, at, :], term)
        came = got[c * each][...]
        if each == 2:
            came = jnp.where(s_ref[4] > 0, got[c * each + 1][...], came)
        came = jnp.where(s_ref[2] > 0, came.astype(F32), 0.0)
        out_ref[at, :] = (came + jnp.where(s_ref[3] > 0, term, 0.0)).astype(BF16)


def payload(scalars, got, parts, hidden, rows_at, *after):
    part, hid = got[0].shape
    rows = part * parts
    step = block_of(hid, 3584)
    grid_spec = pltpu.PrefetchScalarGridSpec(
        num_scalar_prefetch=1,
        grid=(hid // step,),
        in_specs=[pl.BlockSpec((part, step), lambda i, s: (0, i))] * len(got)
        + [
            pl.BlockSpec((1, rows, step), lambda i, s, j=j: (s[j], rows_at[j] // rows, i))
            for j in range(len(hidden))
        ]
        + [ANYWHERE] * len(after),
        out_specs=pl.BlockSpec((rows, step), lambda i, s: (0, i)),
    )

    def kernel(*refs):
        payload_kernel(len(got), len(hidden), *refs)

    return pl.pallas_call(
        kernel,
        grid_spec=grid_spec,
        out_shape=jax.ShapeDtypeStruct((rows, hid), BF16),
        compiler_params=pltpu.CompilerParams(vmem_limit_bytes=PAYLOAD_LIMIT << 20),
        cost_estimate=SHORT,
        name="payload",
    )(scalars, *got, *hidden, *after)


def first_kernel(n, cores, s_ref, own_gate, proj, *refs):
    group = n // cores
    held, out_ref = refs[-2 - group : -2], refs[-1]
    gates = [
        jnp.concatenate([ref[...] for ref in refs[i * CHUNKS : (i + 1) * CHUNKS]])
        for i in range(2 * n - 2)
    ]

    @pl.when(pl.program_id(0) == 0)
    def _():
        out_ref[...] = jnp.zeros_like(out_ref)

    for k in range(n):
        if k:
            up, down = gates[2 * k - 2 : 2 * k], gates[2 * (n - 1 - k) : 2 * (n - k)]
            below = up[0] if k == 1 else jnp.where(s_ref[n] > 0, up[0], up[1])
            above = down[1] if k == n - 1 else jnp.where(s_ref[n] > 0, down[1], down[0])
            gate = jnp.where(s_ref[n + k] > 0, below, above)
        else:
            gate = own_gate[...]
        hidden = held[k % group][0]
        for e in range(1, cores):
            hidden = jnp.where(s_ref[k] == e, held[k % group][e], hidden)
        high, low = split(hidden * gate.astype(F32))
        out_ref[k] += lax.dot_general(
            proj[...], high, ROWS_ROWS, preferred_element_type=F32
        ) + lax.dot_general(proj[...], low, ROWS_ROWS, preferred_element_type=F32)


def projected_first(n, cores, scalars, gate_act, proj_t, gates, hidden, after):
    part, hid = gates[0].shape
    half = part * CHUNKS
    step = block_of(hid, 512)
    flat = pl.BlockSpec((half, step), lambda i, s: (0, i))
    grid_spec = pltpu.PrefetchScalarGridSpec(
        num_scalar_prefetch=1,
        grid=(hid // step,),
        in_specs=[
            flat,
            pl.BlockSpec((R, step), lambda i, s: (0, i)),
        ]
        + [pl.BlockSpec((part, step), lambda i, s: (0, i))] * len(gates)
        + [pl.BlockSpec((cores, half, step), lambda i, s: (0, 0, i))] * len(hidden)
        + [ANYWHERE],
        out_specs=pl.BlockSpec((n, R, half), lambda i, s: (0, 0, 0)),
    )

    def kernel(*refs):
        first_kernel(n, cores, *refs)

    return pl.pallas_call(
        kernel,
        grid_spec=grid_spec,
        out_shape=jax.ShapeDtypeStruct((n, R, half), F32),
        compiler_params=pltpu.CompilerParams(vmem_limit_bytes=FIRST_LIMIT << 20),
        cost_estimate=cost(16),
        name="projected_first",
    )(scalars, gate_act, proj_t, *gates, *hidden, after)


def inputs_kernel(x_ref, proj_ref, after_ref, out_ref):
    del after_ref
    out_ref[...] = lax.dot_general(
        x_ref[...], proj_ref[...], ROWS_ROWS, preferred_element_type=F32
    )


def projected_inputs(inputs, proj_t, after):
    whole = pl.BlockSpec(memory_space=pltpu.VMEM)
    return pl.pallas_call(
        inputs_kernel,
        in_specs=[whole, whole, ANYWHERE],
        out_specs=whole,
        out_shape=jax.ShapeDtypeStruct((inputs.shape[0], R), F32),
        compiler_params=pltpu.CompilerParams(vmem_limit_bytes=12 << 20),
        cost_estimate=cost(1),
        name="projected_inputs",
    )(inputs, proj_t, after)


def local(grad_out, inputs, gate_act, w_down, proj_in, proj_out, queries, example_of):
    n = lax.axis_size("blk")
    cores = lax.axis_size("sub")
    n_f = lax.axis_size("fsdp")
    z, x, core = lax.axis_index("blk"), lax.axis_index("fsdp"), lax.axis_index("sub")
    tok = grad_out.shape[0]
    hid, dblk = w_down.shape
    group = n // cores
    half = tok // 2

    def features(p):
        part = tok // n_f
        mine = lax.dynamic_slice(grad_out, (x * part, ((z + p) % group) * dblk), (part, dblk))
        route = []
        for zs in range(n):
            for cs in range(cores):
                zd = cs * group + (zs + p) % group
                route.append((zs * cores + cs, zd * cores + zs // group))
        return lax.ppermute(mine, ("blk", "sub"), route)

    def whole_of(got, after):
        parts = [got] + [shifted(got, "fsdp", e) for e in range(1, n_f)]
        return join(parts, x, after)

    def spread(whole):
        return [whole] + [shifted(whole, "sub", e) for e in range(1, cores)]

    def block_at(distance):
        return (core - ((z - distance) % n) // group) % cores

    def needed(step):
        return sorted({step % group, (n - step) % group})

    begin = needed(1)
    later = [p for p in range(group) if p not in begin]
    features_of = {p: features(p) for p in begin + later}
    part = half // CHUNKS
    even = x % 2 == 0
    came = []
    for c in range(CHUNKS):
        own = gate_act[c * part : (c + 1) * part]
        came.append([[line_right(own), line_left(own)]])
    waits = came[0][0] + [features_of[p] for p in later[:1]]
    whole = {p: whole_of(features_of[p], waits) for p in begin}
    spreads = {p: spread(whole[p]) for p in begin}
    last = example_of
    second, first = {}, {}
    for p in begin:
        last = hidden_grad(spreads[p], w_down, half, half, last)
        second[p] = (last, 0)
    last, all_q = list(came[-1][0]), None

    width = R * R // cores

    def all_queries(after):
        own_q = block_copy(queries[0], 0 * z, 0 * z, queries.shape[1:], after)
        own_q = own_q.reshape(cores, -1, width)
        got_q = [lax.dynamic_index_in_dim(own_q, core, 0, keepdims=False)]
        for e in range(1, cores):
            got_q.append(
                shifted(lax.dynamic_index_in_dim(own_q, (core + e) % cores, 0, keepdims=False), "sub", e)
            )
        own_q = jnp.concatenate([lax.select_n((core - i) % cores, *got_q) for i in range(cores)], axis=1)
        return gathered(own_q, "blk")

    def counts(rightward):
        return jnp.where(rightward, z > 0, z < n - 1)

    for s in range(1, n):
        parts = [came] if s == n - 1 else [[stream] for stream in came]
        sent = []
        for c, streams in enumerate(parts):
            both = []
            for reverse in (False, True):
                rightward = even != reverse
                right, left = block_at(s), block_at(n - s)
                flags = [
                    counts(rightward),
                    jnp.where(rightward, z < s, z + s >= n),
                    jnp.logical_not(rightward),
                ]
                if s % group == (n - s) % group:
                    which, arrays = [jnp.where(rightward, right, left)] * 2, [second[s % group]]
                else:
                    which, arrays = [right, left], [second[s % group], second[(n - s) % group]]
                scalars = jnp.stack(which + [f.astype(jnp.int32) for f in flags])
                if s == 1:
                    got = [block for stream in streams for block in stream[-1]]
                else:
                    got = [stream[-1][int(reverse)] for stream in streams]
                rows_at = [start + c * part * len(streams) for _, start in arrays]
                arrays = [array for array, _ in arrays]
                if s == 1 and not reverse and c == len(parts) - 1:
                    for p in later:
                        whole[p] = whole_of(features_of[p], last)
                    last = last + [whole[later[0]]]
                last = payload(scalars, got, len(streams), arrays, rows_at, *last)
                last = [last]
                both.append(onward(last[0], reverse))
            sent.append(both)
        if s < n - 1:
            for stream, both in zip(came, sent, strict=True):
                stream.append(both)
        if s == n - 2:
            all_q = all_queries(last[0])
        for p in needed(s + 1):
            if p not in second:
                spreads[p] = spread(whole[p])
                first[p] = hidden_grad(spreads[p], w_down, 0, tok, last[0])
                last, second[p] = [first[p]], (first[p], half)
        if s == n - 2:
            for p in begin:
                first[p] = hidden_grad(spreads[p], w_down, 0, half, last[0])
                last = [first[p]]

    gates = [came[c][s][d] for s in range(n - 1) for d in (0, 1) for c in range(CHUNKS)]
    scalars = [block_at(k) for k in range(n)] + [even] + [z >= k for k in range(1, n)]
    scalars = jnp.stack([f.astype(jnp.int32) for f in scalars])
    ups = projected_first(
        n,
        cores,
        scalars,
        gate_act,
        proj_out.T,
        gates,
        [first[p] for p in range(group)],
        last[0],
    )
    up_first = ups[0]
    for k in range(1, n):
        up_first = up_first + shifted(ups[k], "blk", -k)

    own_second = lax.dynamic_index_in_dim(second[0][0], block_at(0), 0, keepdims=False)[second[0][1] :]
    total = own_second + sum(
        jnp.where(counts(even != bool(d)), sent[0][d].astype(F32), 0.0) for d in (0, 1)
    )
    up_second = lax.dot_general(
        proj_out.astype(F32),
        total * gate_act[half:].astype(F32),
        (((0,), (1,)), ((), ())),
        precision=lax.Precision.HIGH,
        preferred_element_type=F32,
    )
    up_proj = summed(jnp.concatenate([up_first, up_second], axis=1), ("sub", "fsdp"))

    left_proj = summed(projected_inputs(inputs, proj_in.T, ups), ("sub", "fsdp"))
    onehot = (example_of[:, None] == jnp.arange(EX_DEV, dtype=jnp.int32)[None, :]).astype(F32)
    weighted = (onehot[:, :, None] * left_proj[:, None, :]).reshape(tok, EX_DEV * R)
    full_sketch = lax.dot_general(
        weighted, up_proj, (((0,), (1,)), ((), ())), precision=lax.Precision.HIGHEST
    )
    sketch = full_sketch.reshape(EX_DEV, R * R).astype(BF16)
    sketch_part = lax.dynamic_slice(sketch, (0, core * width), (EX_DEV, width))
    scores = lax.dot_general(
        sketch, all_q, (((1,), (2,)), ((), ())), preferred_element_type=F32
    )
    return sketch_part, scores


def solution(mesh):
    in_specs = (
        P(("groups", "blk"), "sub"),
        P(("groups", "blk"), ("fsdp", "sub")),
        P(("groups", "blk"), ("fsdp", "sub")),
        P(("fsdp", "sub"), "blk"),
        P(("fsdp", "sub"), None),
        P(("fsdp", "sub"), None),
        P(("groups", "blk"), "fsdp", "sub"),
        P(("groups", "blk")),
    )
    out_specs = (P(("groups", "blk"), "sub"), P(("groups", "blk"), None, ("fsdp", "sub")))
    return jax.shard_map(local, mesh=mesh, in_specs=in_specs, out_specs=out_specs, check_vma=False)
```
